128 devices in a mesh: sub: 32 (over y_hi, x, z), freq: 4 (over y_lo, core).
Axes of the slice: x: 4, y: 4 (y_hi: 2, y_lo: 2; y = y_hi * 2 + y_lo), z: 4, core: 2. Of those that a mesh axis runs over, the one named last changes fastest.
Arguments:
- z_vectors: bfloat16 [1572864, 64], P(('freq', 'sub')), parts along dimension 0, may hold values from -0.0546875 to 0.0546875
- band_tiles: bfloat16 [8, 3072, 3, 128, 128], P('freq', 'sub'), parts along dimension 0, may hold values from -6 to 6
- coupling_tiles: bfloat16 [8, 192, 512, 512], P('freq', 'sub'), parts along dimension 0, may hold values from -24 to 24
- neighbours: int32 [32, 6], P('sub'), may hold values from 0 to 31, as said below
- interface_rows: int32 [32, 6, 512], P('sub'), may hold values from 0 to 12287
- coarse_number: int32 [32], replicated, may hold values from 0 to 31, each once
Outputs:
- coarse: float32 [8, 2048, 2048], P('freq', 'sub'), parts along dimension 0
The draws below stay inside these ranges and needn't reach their ends.
There are 4 independent parts, one for each index of `freq`. The reference program is written for one: setup_inputs(seed, part) draws one part's arguments, and reference() takes and returns one part's arrays. A program takes and returns all parts, laid end to end along the dimension named above; an argument that names none is the same for every part. Nothing has to cross between parts.
Inputs may be any that keep to these rules, and one draw needn't show every extreme that they name: The neighbours of a subdomain are 6 distinct subdomains other than itself, and if t is in slot j of s then s is in slot 5 - j of t.
All inputs are finite; a program needn't handle non-finite values.
Results may differ from the reference program's by a relative error of at most 0.0029.
Values may be sent and summed in bfloat16 or wider, within the bound.
No kernel may reach another device: no remote copies, remote signals or barrier semaphores. Data moves between devices by JAX's collectives and lax.ppermute only.
A program may use at most 128 MiB of HBM per device.

```python
import jax
import jax.numpy as jnp
from jax import lax

K = 64
BLK = 128
NBLK = 96
NB = 6
IF = 512
SUBS = 32
ROWS = 12288


def draw_neighbours(key, part):
    order = jax.random.permutation(key, SUBS).astype(jnp.int32)
    place = jnp.argsort(order).astype(jnp.int32)
    half = NB // 2
    offsets = jnp.concatenate([jnp.arange(-half, 0, dtype=jnp.int32), jnp.arange(1, half + 1, dtype=jnp.int32)])
    return order[(place[:, None] + offsets[None, :]) % SUBS].astype(jnp.int32)


def touch_ends(array, own_key, low, largest):
    index_at = [jax.random.randint(jax.random.fold_in(own_key, axis), (), 0, length) for axis, length in enumerate(array.shape)]
    widest = array.shape.index(max(array.shape))
    next_to = index_at[:widest] + [(index_at[widest] + 1) % array.shape[widest]] + index_at[widest + 1:]
    return array.at[tuple(index_at)].set(low).at[tuple(next_to)].set(largest)


def shard_levels(own_key, extent, cuts, low, largest):
    level, own = 1.0, jax.random.fold_in(own_key, 6)
    for position, blocks in cuts:
        draws = jnp.exp(jax.random.uniform(jax.random.fold_in(own, position), (blocks,), jnp.float32, low / len(cuts), largest / len(cuts)))
        level = level * jnp.repeat(draws, extent[position] // blocks).reshape([-1 if axis == position else 1 for axis in range(len(extent))])
    return level


def gaussian(own_key, shape, spread, reach, split=(), held_as=jnp.bfloat16):
    array = jax.random.normal(own_key, shape, jnp.float32) * spread
    if len(split) > 0:
        array = shard_levels(own_key, shape, split, -0.22, 0.18) * array
    return jnp.clip(array, min=-reach, max=reach).astype(held_as)


def setup_inputs(seed: int = 0, part: int = 0) -> dict:
    streams_of = jax.random.split(jax.random.key(seed), 7)
    own_keys = jax.random.split(jax.random.fold_in(streams_of[6], part), 7)
    return {
        "z_vectors": gaussian(own_keys[0], (SUBS * ROWS, K), ROWS ** -0.5, 0.0546875, ((0, 32),)),
        "band_tiles": gaussian(own_keys[1], (2, SUBS * NBLK, 3, BLK, BLK), 1.0, 6.0, ((1, 32),)),
        "coupling_tiles": gaussian(own_keys[2], (2, SUBS * NB, IF, IF), 4.0, 24.0, ((1, 32),)),
        "neighbours": draw_neighbours(jax.random.fold_in(streams_of[6], 71), part),
        "interface_rows": touch_ends(jax.random.randint(streams_of[4], (SUBS, NB, IF), 0, ROWS), jax.random.fold_in(streams_of[4], 1), 0, ROWS - 1).astype(jnp.int32),
        "coarse_number": jax.random.permutation(streams_of[5], SUBS).astype(jnp.int32),
    }


def one_subdomain(packed):
    zs, tiles, coup, rows_s, remote, cols = packed
    hp = lax.Precision.HIGHEST
    zb = zs.reshape(NBLK, BLK, K)
    zpad = jnp.pad(zb, ((1, 1), (0, 0), (0, 0)))
    zshift = jnp.stack([zpad[0:NBLK], zpad[1:NBLK + 1], zpad[2:NBLK + 2]], axis=1)
    image = jnp.einsum("rbkij,bkjn->rbin", tiles.astype(jnp.float32), zshift.astype(jnp.float32), precision=hp)
    image = image.astype(jnp.bfloat16)
    diag_block = jnp.einsum("bin,rbim->rnm", zb.astype(jnp.float32), image.astype(jnp.float32), precision=hp)
    cross = jnp.einsum("rjab,jbn->rjan", coup.astype(jnp.float32), remote.astype(jnp.float32), precision=hp)
    cross = cross.astype(jnp.bfloat16)
    local_rows = zs[rows_s.reshape(-1)].reshape(NB, IF, K)
    off_block = jnp.einsum("jan,rjam->rjnm", local_rows.astype(jnp.float32), cross.astype(jnp.float32), precision=hp)
    blocks = jnp.concatenate([diag_block[:, None], off_block], axis=1)
    onehot = (cols[:, None] == jnp.arange(SUBS, dtype=jnp.int32)[None, :]).astype(jnp.float32)
    row = jnp.einsum("js,rjnm->rnsm", onehot, blocks, precision=hp)
    return row.reshape(2, K, SUBS * K)


def reference(z_vectors, band_tiles, coupling_tiles, neighbours, interface_rows, coarse_number):
    zall = z_vectors.reshape(SUBS, ROWS, K)
    tiles = jnp.moveaxis(band_tiles.reshape(2, SUBS, NBLK, 3, BLK, BLK), 1, 0)
    coup = jnp.moveaxis(coupling_tiles.reshape(2, SUBS, NB, IF, IF), 1, 0)
    back_rows = interface_rows[neighbours, jnp.arange(NB - 1, -1, -1, dtype=jnp.int32)[None, :]]
    remote = zall[neighbours[:, :, None], back_rows]
    cols = jnp.concatenate([coarse_number[:, None], coarse_number[neighbours]], axis=1).astype(jnp.int32)
    rows_all = lax.map(one_subdomain, (zall, tiles, coup, interface_rows, remote, cols))
    return jnp.moveaxis(rows_all, 1, 0).reshape(2, SUBS * K, SUBS * K)
```

```python
import functools

import jax
import jax.numpy as jnp
from jax import lax
from jax.experimental import pallas as pl
from jax.experimental.pallas import tpu as pltpu
from jax.sharding import PartitionSpec as P

GROUP = 1024


def gather_kernel(nbr_ref, rows_ref, z_ref, send_ref, local_ref, stack, sems):
    width, count = z_ref.shape
    slots, _, span = rows_ref.shape
    groups = count // GROUP
    for g in range(groups):
        stack[g * width : (g + 1) * width, :] = z_ref[:, g * GROUP : (g + 1) * GROUP]
    local_iota = lax.broadcasted_iota(jnp.int32, (GROUP, span), 0)

    def step(j, carry):
        rows = rows_ref[j]
        low = rows % GROUP
        group = rows // GROUP
        onehot = jnp.where(local_iota == low, 1.0, 0.0).astype(jnp.bfloat16)
        found = jnp.dot(stack[...], onehot, preferred_element_type=jnp.float32)
        picked = found[0:width]
        for g in range(1, groups):
            picked = jnp.where(group == g, found[g * width : (g + 1) * width], picked)
        local_ref[j] = picked.astype(jnp.bfloat16)
        pltpu.make_async_copy(local_ref.at[j], send_ref.at[nbr_ref[j]], sems.at[j]).start()
        return carry

    lax.fori_loop(0, slots, step, 0)
    for j in range(slots):
        pltpu.make_async_copy(local_ref.at[j], send_ref.at[nbr_ref[j]], sems.at[j]).wait()


def final_kernel(nbr_ref, col_ref, me_ref, recv_ref, y_ref, diag_ref, out_ref, held, sems):
    slots, _, span = y_ref.shape
    width = diag_ref.shape[1]

    def fetch(j):
        return pltpu.make_async_copy(recv_ref.at[nbr_ref[j]], held.at[j], sems.at[j])

    for j in range(slots):
        fetch(j).start()
    out_ref[...] = jnp.zeros_like(out_ref)
    upper = lax.broadcasted_iota(jnp.int32, (width, 2 * width), 1) // width

    def place(r, col, value):
        where = pl.ds(pl.multiple_of((col // 2) * 2 * width, 2 * width), 2 * width)
        out_ref[r, :, where] += jnp.where(upper == col % 2, value, 0.0)

    own = col_ref[me_ref[0]]
    for r in range(2):
        value = diag_ref[r]
        place(r, own, jnp.concatenate([value, value], axis=1))
    for j in range(slots):
        fetch(j).wait()
        far = held[j]
        both = lax.dot_general(
            y_ref[j],
            jnp.concatenate([far, far], axis=0),
            (((1,), (1,)), ((), ())),
            preferred_element_type=jnp.float32,
        )
        col = col_ref[nbr_ref[j]]
        for r in range(2):
            high = both[2 * r * width : (2 * r + 1) * width]
            low = both[(2 * r + 1) * width : (2 * r + 2) * width]
            place(r, col, high + low)


def body(z_vectors, band_tiles, coupling_tiles, neighbours, interface_rows, coarse_number):
    count, width = z_vectors.shape
    slots = neighbours.shape[1]
    span = interface_rows.shape[2]
    nblocks = band_tiles.shape[1]
    tile_rows = band_tiles.shape[-1]
    sub_count = lax.axis_size("sub")
    myself = lax.axis_index("sub")
    nbrs = neighbours[0]
    smem = pl.BlockSpec(memory_space=pltpu.SMEM)
    vmem = pl.BlockSpec(memory_space=pltpu.VMEM)
    anywhere = pl.BlockSpec(memory_space=pl.ANY)
    send, local = pl.pallas_call(
        gather_kernel,
        out_shape=(
            jax.ShapeDtypeStruct((sub_count, width, span), jnp.bfloat16),
            jax.ShapeDtypeStruct((slots, width, span), jnp.bfloat16),
        ),
        in_specs=[smem, vmem, vmem],
        out_specs=(anywhere, vmem),
        scratch_shapes=[
            pltpu.VMEM((count // GROUP * width, GROUP), jnp.bfloat16),
            pltpu.SemaphoreType.DMA((slots,)),
        ],
        compiler_params=pltpu.CompilerParams(vmem_limit_bytes=32 * 1024 * 1024),
    )(nbrs, interface_rows[0][:, None, :], z_vectors.T)
    recv = lax.all_to_all(send, "sub", 0, 0, tiled=True)

    zblocks = z_vectors.reshape(nblocks, tile_rows, width)
    zpad = jnp.pad(zblocks, ((1, 1), (0, 0), (0, 0)))
    zshift = jnp.stack([zpad[0:nblocks], zpad[1 : nblocks + 1], zpad[2 : nblocks + 2]], axis=1)
    image = jnp.einsum(
        "rbkij,bkjn->rbin", band_tiles, zshift, preferred_element_type=jnp.float32
    ).astype(jnp.bfloat16)
    diag_block = jnp.einsum("bin,rbim->rnm", zblocks, image, preferred_element_type=jnp.float32)
    y = jnp.einsum("jna,rjab->jrnb", local, coupling_tiles, preferred_element_type=jnp.float32)
    y_high = lax.reduce_precision(y, 8, 7)
    y_low = (y - y_high).astype(jnp.bfloat16)
    y_high = y_high.astype(jnp.bfloat16)
    y_both = jnp.stack([y_high, y_low], axis=2).reshape(slots, 4 * width, span)

    return pl.pallas_call(
        final_kernel,
        out_shape=jax.ShapeDtypeStruct((2, width, sub_count * width), jnp.float32),
        in_specs=[smem, smem, smem, anywhere, vmem, vmem],
        out_specs=vmem,
        scratch_shapes=[
            pltpu.VMEM((slots, width, span), jnp.bfloat16),
            pltpu.SemaphoreType.DMA((slots,)),
        ],
        compiler_params=pltpu.CompilerParams(vmem_limit_bytes=32 * 1024 * 1024),
    )(nbrs, coarse_number, myself.astype(jnp.int32)[None], recv, y_both, diag_block)


def solution(mesh):
    in_specs = (
        P(("freq", "sub"), None),
        P("freq", "sub", None, None, None),
        P("freq", "sub", None, None),
        P("sub", None),
        P("sub", None, None),
        P(),
    )
    out_specs = P("freq", "sub", None)
    return jax.shard_map(body, mesh=mesh, in_specs=in_specs, out_specs=out_specs, check_vma=False)
```
